32 devices in a mesh: parts: 2 (over y), wide: 4 (over z), col: 2 (over x), sub: 2 (over core).
Axes of the slice: x: 2, y: 2, z: 4, core: 2. Of those that a mesh axis runs over, the one named last changes fastest.
Arguments:
- parent_inverse: float32 [16384, 8192], P(('parts', 'wide'), 'col'), parts along dimension 0, as said below
- child_rows: int32 [4, 3072], P(('parts', 'sub')), parts along dimension 0, may hold values from 0 to 2047, as said below
- row_counts: int32 [4, 4], P(('parts', 'sub')), parts along dimension 0, may hold values from 1 to 768, as said below
- child_factor: float32 [4, 3072, 6144], P(('parts', 'sub'), 'wide', 'col'), parts along dimension 0, may hold values from -0.21875 to 0.21875
- own_variance: float32 [4, 6144], P(('parts', 'sub'), 'col'), parts along dimension 0, may hold values from 0.5 to 2
Outputs:
- cross_block: float32 [4, 3072, 6144], P(('parts', 'sub'), 'wide', 'col'), parts along dimension 0
- variances: float32 [4, 6144], P(('parts', 'sub'), 'col'), parts along dimension 0
The draws below stay inside these ranges and needn't reach their ends.
There are 2 independent parts, one for each index of `parts`. The reference program is written for one: setup_inputs(seed, part) draws one part's arguments, and reference() takes and returns one part's arrays. A program takes and returns all parts, laid end to end along the dimension named above; each array names one. Nothing has to cross between parts.
Inputs may be any that keep to these rules, and one draw needn't show every extreme that they name: `child_rows`: within each child and block, the live slots hold distinct offsets. `row_counts`: each child has at least one block with all 768 slots live. `parent_inverse`: Symmetric.
All inputs are finite; a program needn't handle non-finite values.
Results may differ from the reference program's by a relative error of at most 0.0001.
Values sent between devices are 32-bit elements; how exact they have to be, the bound alone decides.
A program may use at most 320 MiB of HBM per device.

```python
import math
import jax
import jax.numpy as jnp
from jax import lax

P_SIZE = 8192
S = 3072
NC = 6144
CHILDREN = 2
PB = 2048
RB = 768


def draw_parent_inverse(key, part):
    key = jax.random.fold_in(key, 11)
    noise_key, diagonal_key = jax.random.split(key, 2)
    noise = jax.random.normal(noise_key, (P_SIZE, P_SIZE), jnp.float32)
    coupling = (noise + noise.T) * (0.4 / math.sqrt(2.0 * P_SIZE))
    diagonal = jnp.exp(jax.random.uniform(diagonal_key, (P_SIZE,), jnp.float32, 0.0, math.log(2.0)))
    identity = jnp.arange(P_SIZE)[:, None] == jnp.arange(P_SIZE)[None, :]
    result = coupling + jnp.where(identity, diagonal[:, None], 0.0)
    return result.astype(jnp.float32)


def draw_child_rows(key, part):
    key = jax.random.fold_in(key, 5)
    subkeys = jax.random.split(key, CHILDREN * (S // RB))
    chosen = jax.vmap(lambda single: jax.random.permutation(single, PB)[:RB])(subkeys)
    return chosen.reshape(CHILDREN, S).astype(jnp.int32)


def draw_row_counts(key, part):
    key = jax.random.fold_in(key, 7)
    first_key, second_key = jax.random.split(key)
    drawn = jax.random.randint(first_key, (CHILDREN, S // RB), 1, RB + 1)
    filled_block = jax.random.randint(second_key, (CHILDREN, 1), 0, S // RB)
    blocks_index = jnp.arange(S // RB)[None, :]
    return jnp.where(blocks_index == filled_block, RB, drawn).astype(jnp.int32)


def level_of(stream_key, dims, cuts, least, largest):
    def one(position, parts):
        heights = jax.random.uniform(jax.random.fold_in(jax.random.fold_in(stream_key, 6), position), (parts,), jnp.float32, least / len(cuts), largest / len(cuts))
        return jnp.repeat(jnp.exp(heights), dims[position] // parts).reshape((-1,) + (1,) * (len(dims) - position - 1))

    gain = one(*cuts[0])
    for cut in cuts[1:]:
        gain = gain * one(*cut)
    return gain


def gaussian(rng, extent, width, limit, pieces=(), held_as=jnp.bfloat16):
    values = jax.random.normal(rng, extent, jnp.float32) * width
    if len(pieces) > 0:
        values = level_of(rng, extent, pieces, -0.22, 0.18) * values
    return jnp.clip(values, min=-limit, max=limit).astype(held_as)


def setup_inputs(seed: int = 0, part: int = 0) -> dict:
    streams_of = jax.random.split(jax.random.key(seed), 6)
    own_keys = jax.random.split(jax.random.fold_in(streams_of[5], part), 6)
    parent_inverse = draw_parent_inverse(jax.random.fold_in(jax.random.fold_in(streams_of[5], part), 71), part)
    child_rows = draw_child_rows(jax.random.fold_in(jax.random.fold_in(streams_of[5], part), 71), part)
    row_counts = draw_row_counts(jax.random.fold_in(jax.random.fold_in(streams_of[5], part), 71), part)
    child_factor = gaussian(own_keys[3], (CHILDREN, S, NC), (S // 4) ** -0.5, 0.21875, ((0, 2), (1, 4), (2, 2)), jnp.float32)
    own_variance = jnp.clip(jnp.exp(math.log(2.0) - 1.3862944 * jax.random.uniform(own_keys[4], (CHILDREN, NC), jnp.float32) ** level_of(own_keys[4], (CHILDREN, NC), ((0, 2), (1, 2)), -0.2, 0.2)), 0.5, 2.0)
    return dict(parent_inverse=parent_inverse, child_rows=child_rows, row_counts=row_counts, child_factor=child_factor, own_variance=own_variance)


def reference(parent_inverse, child_rows, row_counts, child_factor, own_variance):
    blocks = S // RB
    offsets = (jnp.arange(blocks, dtype=jnp.int32) * PB)[:, None]
    slot_index = jnp.arange(RB, dtype=jnp.int32)
    cross_list = []
    variance_list = []
    for child_index in range(CHILDREN):
        global_rows = (offsets + child_rows[child_index].reshape(blocks, RB)).reshape(S).astype(jnp.int32)
        live_rows = (slot_index[None, :] < row_counts[child_index][:, None]).reshape(S)
        sigma_rows = parent_inverse[global_rows][:, global_rows]
        sigma_rows = jnp.where(live_rows[:, None] & live_rows[None, :], sigma_rows, jnp.zeros_like(sigma_rows))
        cross_part = -jnp.dot(sigma_rows, child_factor[child_index], precision=lax.Precision.HIGHEST, preferred_element_type=jnp.float32)
        cross_list.append(cross_part)
        variance_list.append(own_variance[child_index] - jnp.sum(child_factor[child_index] * cross_part, axis=0))
    return jnp.stack(cross_list), jnp.stack(variance_list)
```

```python
import jax
import jax.numpy as jnp
from jax import lax
from jax.sharding import PartitionSpec as P

PIPES = 2


def dot(a, b, contract):
    return lax.dot_general(
        a,
        b,
        ((contract[0], contract[1]), ((), ())),
        precision=lax.Precision.HIGH,
        preferred_element_type=jnp.float32,
    )


def per_device(parent_inverse, child_rows, row_counts, child_factor, own_variance):
    wide = lax.axis_size("wide")
    cols = lax.axis_size("col")
    me = lax.axis_index("wide")
    my_col = lax.axis_index("col")
    slots, width = child_factor.shape[1:]
    block_rows, block_cols = parent_inverse.shape
    held = block_cols // block_rows
    factor = child_factor[0]
    offsets = child_rows[0].reshape(wide, slots)
    slot_index = jnp.arange(slots, dtype=jnp.int32)
    half = width // 2
    pipe = half // PIPES
    right = [(i, i + 1) for i in range(wide - 1)]
    left = [(i + 1, i) for i in range(wide - 1)]
    ways = ((me, right, -1), (wide - 1 - me, left, 1))

    spread = [factor[:, p * pipe : (p + 1) * pipe] for p in range(PIPES)]
    summed = factor[:, half:]
    got = [[lax.ppermute(spread[p], "wide", perm) for _, perm, _ in ways] for p in range(PIPES)]

    mine = lax.dynamic_index_in_dim(offsets, me, 0, keepdims=False)
    live_mine = slot_index < lax.dynamic_index_in_dim(row_counts[0], me, 0, keepdims=False)
    local_rows = jnp.where(live_mine[:, None], parent_inverse[mine], 0.0)
    high = lax.reduce_precision(local_rows, 8, 7)
    low = (local_rows - high).astype(jnp.bfloat16)
    high = high.astype(jnp.bfloat16)
    flip = jnp.where(me < wide // 2, held - 1, 0)
    pieces = []
    for i in range(held):
        at = jnp.where(flip > 0, held - 1 - i, i)
        block = my_col * held + at
        offset = lax.dynamic_index_in_dim(offsets, block, 0, keepdims=False)
        live = slot_index < lax.dynamic_index_in_dim(row_counts[0], block, 0, keepdims=False)
        pick = (
            (jnp.arange(block_rows, dtype=jnp.int32)[:, None] == offset[None, :]) & live[None, :]
        ).astype(jnp.bfloat16)
        piece = 0.0
        for part in (low, high):
            columns = lax.dynamic_slice_in_dim(part, at * block_rows, block_rows, 1)
            piece += jnp.dot(columns, pick, preferred_element_type=jnp.float32)
        pieces.append(lax.all_gather(piece, "col", axis=0))

    def sigma(block, valid):
        owner = block // held
        at = block % held
        order = jnp.where(flip > 0, held - 1 - at, at)
        value = lax.dynamic_index_in_dim(pieces[0], owner, 0, keepdims=False)
        for i in range(1, held):
            other = lax.dynamic_index_in_dim(pieces[i], owner, 0, keepdims=False)
            value = jnp.where(order == i, other, value)
        return jnp.where(valid, value, 0.0)

    own = sigma(me, True)
    total = [dot(own, spread[p], ((1,), (0,))) for p in range(PIPES)]
    finish = dot(own, summed, ((1,), (0,)))
    for step in range(2, wide + 1):
        for w, (rank, perm, sign) in enumerate(ways):
            source = me + sign * (step - 1)
            here = sigma(jnp.clip(source, 0, wide - 1), rank >= step - 1)
            target = me - sign * (wide - step + 1)
            away = sigma(jnp.clip(target, 0, wide - 1), rank <= step - 2)
            terms = dot(away, summed, ((0,), (0,)))
            for p in range(PIPES):
                came = got[p][w]
                total[p] += dot(here, came, ((1,), (0,)))
                send = came + terms[:, p * pipe : (p + 1) * pipe]
                got[p][w] = lax.ppermute(send, "wide", perm)
    parts = [-t for t in total]
    for p in range(PIPES):
        parts.append(-(finish[:, p * pipe : (p + 1) * pipe] + got[p][0] + got[p][1]))
    cross_part = jnp.concatenate(parts, axis=1)
    partial_value = jnp.sum(factor * cross_part, axis=0)
    totals = lax.psum(partial_value, "wide")
    return (cross_part[None], (own_variance[0] - totals)[None])


def solution(mesh):
    placed = (
        P(("parts", "wide"), "col"),
        P(("parts", "sub"), None),
        P(("parts", "sub"), None),
        P(("parts", "sub"), "wide", "col"),
        P(("parts", "sub"), "col"),
    )
    return jax.shard_map(
        per_device,
        mesh=mesh,
        in_specs=placed,
        out_specs=(P(("parts", "sub"), "wide", "col"), P(("parts", "sub"), "col")),
        check_vma=False,
    )
```

```python
import functools

import jax
import jax.numpy as jnp
from jax import lax
from jax.experimental import pallas as pl
from jax.experimental.pallas import tpu as pltpu
from jax.experimental.layout import Layout, with_layout_constraint
from jax.sharding import PartitionSpec as P

PIPES = 2


def pick_kernel(at_ref, mine_ref, live_ref, wanted_ref, parent_ref, *rest):
    out, rows, sem = rest[-3:]
    slots, block_rows = rows.shape
    columns = pl.ds(pl.multiple_of(at_ref[0] * block_rows, 128), block_rows)

    def issue(i, carry):
        pltpu.make_async_copy(
            parent_ref.at[pl.ds(mine_ref[i], 1), columns], rows.at[pl.ds(i, 1)], sem
        ).start()
        return carry

    lax.fori_loop(0, slots, issue, 0, unroll=8)
    pltpu.make_async_copy(parent_ref.at[pl.ds(0, slots), columns], rows, sem).wait()
    depth = 512 if block_rows % 512 == 0 else block_rows
    out[...] = jnp.zeros_like(out)

    def add(c, carry):
        x = rows[:, pl.ds(pl.multiple_of(c * depth, 128), depth)]
        high = x.astype(jnp.bfloat16)
        low = (x - high.astype(jnp.float32)).astype(jnp.bfloat16)
        place = lax.broadcasted_iota(jnp.int32, (depth, slots), 0) + c * depth
        pick = jnp.where(place == wanted_ref[...], 1.0, 0.0).astype(jnp.bfloat16)
        out[...] += jnp.dot(low, pick, preferred_element_type=jnp.float32) + jnp.dot(
            high, pick, preferred_element_type=jnp.float32
        )
        return carry

    lax.fori_loop(0, block_rows // depth, add, 0)
    out[...] = jnp.where(live_ref[...] > 0.0, out[...], 0.0)


def dot(a, b, contract):
    return lax.dot_general(
        a,
        b,
        ((contract[0], contract[1]), ((), ())),
        precision=lax.Precision.HIGH,
        preferred_element_type=jnp.float32,
    )


def per_device(parent_inverse, child_rows, row_counts, child_factor, own_variance):
    wide = lax.axis_size("wide")
    cols = lax.axis_size("col")
    me = lax.axis_index("wide")
    my_col = lax.axis_index("col")
    slots, width = child_factor.shape[1:]
    block_rows, block_cols = parent_inverse.shape
    held = block_cols // block_rows
    factor = child_factor[0]
    offsets = child_rows[0].reshape(wide, slots)
    slot_index = jnp.arange(slots, dtype=jnp.int32)
    half = width // 2
    pipe = half // PIPES
    right = [(i, i + 1) for i in range(wide - 1)]
    left = [(i + 1, i) for i in range(wide - 1)]
    ways = ((me, right, -1), (wide - 1 - me, left, 1))

    def flat(x):
        return with_layout_constraint(x, Layout(major_to_minor=(0, 1)))

    spread = [flat(factor[:, p * pipe : (p + 1) * pipe]) for p in range(PIPES)]
    summed = factor[:, half:]
    got = [[flat(lax.ppermute(spread[p], "wide", perm)) for _, perm, _ in ways] for p in range(PIPES)]

    mine = lax.dynamic_index_in_dim(offsets, me, 0, keepdims=False)
    live_mine = slot_index < lax.dynamic_index_in_dim(row_counts[0], me, 0, keepdims=False)
    flip = jnp.where(me < wide // 2, held - 1, 0)
    at = jnp.stack([jnp.where(flip > 0, held - 1 - i, i) for i in range(held)]).astype(jnp.int32)
    block = my_col * held + at
    wanted = jnp.where(slot_index[None, :] < row_counts[0][block][:, None], offsets[block], -1)
    pieces = []
    for i in range(held):
        local = pl.pallas_call(
            pick_kernel,
            out_shape=jax.ShapeDtypeStruct((slots, slots), jnp.float32),
            in_specs=[
                pl.BlockSpec(memory_space=pltpu.SMEM),
                pl.BlockSpec(memory_space=pltpu.SMEM),
                pl.BlockSpec(memory_space=pltpu.VMEM),
                pl.BlockSpec(memory_space=pltpu.VMEM),
            ]
            + [pl.BlockSpec(memory_space=pl.ANY)] * (1 + PIPES),
            out_specs=pl.BlockSpec(memory_space=pltpu.VMEM),
            scratch_shapes=[pltpu.VMEM((slots, block_rows), jnp.float32), pltpu.SemaphoreType.DMA],
            compiler_params=pltpu.CompilerParams(vmem_limit_bytes=32 * 1024 * 1024),
            cost_estimate=pl.CostEstimate(flops=1000, bytes_accessed=1000, transcendentals=0),
            name="pick",
        )(
            at[i : i + 1],
            mine,
            live_mine.astype(jnp.float32)[:, None],
            wanted[i : i + 1],
            parent_inverse,
            *spread,
        )
        if i == 1:
            corner = sum(jnp.abs(x[0, 0]) for pair in got for x in pair)
            corner = jnp.minimum(corner.astype(jnp.int32), 0)
            local = jnp.where(corner >= 0, local, 0.0)
        pieces.append(lax.all_gather(local, "col", axis=0))
    blocks = jnp.concatenate(pieces, axis=0)

    def sigma(block):
        block = jnp.clip(block, 0, wide - 1)
        at = block % held
        order = jnp.where(flip > 0, held - 1 - at, at)
        return lax.dynamic_index_in_dim(blocks, order * cols + block // held, 0, keepdims=False)

    own = sigma(me)
    total = [dot(own, spread[p], ((1,), (0,))) for p in range(PIPES)]
    finish = dot(own, summed, ((1,), (0,)))
    for step in range(2, wide + 1):
        for w, (rank, perm, sign) in enumerate(ways):
            here = sigma(me + sign * (step - 1))
            target = me - sign * (wide - step + 1)
            if step == 2:
                owner = jnp.clip(target, 0, wide - 1) // held
                away = lax.dynamic_index_in_dim(pieces[0], owner, 0, keepdims=False)
            else:
                away = sigma(target)
            terms = dot(away, summed, ((0,), (0,)))
            for p in range(PIPES):
                came = got[p][w]
                term = terms[:, p * pipe : (p + 1) * pipe]
                send = flat(came + jnp.where(rank <= step - 2, term, 0.0))
                got[p][w] = flat(lax.ppermute(send, "wide", perm))
                total[p] += jnp.where(rank >= step - 1, dot(here, came, ((1,), (0,))), 0.0)
    parts = [-t for t in total]
    for p in range(PIPES):
        parts.append(-(finish[:, p * pipe : (p + 1) * pipe] + got[p][0] + got[p][1]))
    cross_part = jnp.concatenate(parts, axis=1)
    partial_value = jnp.sum(factor * cross_part, axis=0)
    totals = lax.psum(partial_value, "wide")
    return (cross_part[None], (own_variance[0] - totals)[None])


def solution(mesh):
    placed = (
        P(("parts", "wide"), "col"),
        P(("parts", "sub"), None),
        P(("parts", "sub"), None),
        P(("parts", "sub"), "wide", "col"),
        P(("parts", "sub"), "col"),
    )
    return jax.shard_map(
        per_device,
        mesh=mesh,
        in_specs=placed,
        out_specs=(P(("parts", "sub"), "wide", "col"), P(("parts", "sub"), "col")),
        check_vma=False,
    )
```

```python
import functools

import jax
import jax.numpy as jnp
from jax import lax
from jax.experimental import pallas as pl
from jax.experimental.pallas import tpu as pltpu
from jax.experimental.layout import Layout, with_layout_constraint
from jax.sharding import PartitionSpec as P

PIPES = 2


def pick_kernel(at_ref, mine_ref, live_ref, wanted_ref, parent_ref, *rest):
    out, rows, sem = rest[-3:]
    slots, block_rows = rows.shape
    columns = pl.ds(pl.multiple_of(at_ref[0] * block_rows, 128), block_rows)

    def issue(i, carry):
        pltpu.make_async_copy(
            parent_ref.at[pl.ds(mine_ref[i], 1), columns], rows.at[pl.ds(i, 1)], sem
        ).start()
        return carry

    lax.fori_loop(0, slots, issue, 0, unroll=8)
    pltpu.make_async_copy(parent_ref.at[pl.ds(0, slots), columns], rows, sem).wait()
    depth = 512 if block_rows % 512 == 0 else block_rows
    out[...] = jnp.zeros_like(out)

    def add(c, carry):
        x = rows[:, pl.ds(pl.multiple_of(c * depth, 128), depth)]
        high = x.astype(jnp.bfloat16)
        low = (x - high.astype(jnp.float32)).astype(jnp.bfloat16)
        place = lax.broadcasted_iota(jnp.int32, (depth, slots), 0) + c * depth
        pick = jnp.where(place == wanted_ref[...], 1.0, 0.0).astype(jnp.bfloat16)
        out[...] += jnp.dot(low, pick, preferred_element_type=jnp.float32) + jnp.dot(
            high, pick, preferred_element_type=jnp.float32
        )
        return carry

    lax.fori_loop(0, block_rows // depth, add, 0)
    out[...] = jnp.where(live_ref[...] > 0.0, out[...], 0.0)


def dot(a, b, contract):
    return lax.dot_general(
        a,
        b,
        ((contract[0], contract[1]), ((), ())),
        precision=lax.Precision.HIGH,
        preferred_element_type=jnp.float32,
    )


def per_device(parent_inverse, child_rows, row_counts, child_factor, own_variance):
    wide = lax.axis_size("wide")
    cols = lax.axis_size("col")
    me = lax.axis_index("wide")
    my_col = lax.axis_index("col")
    slots, width = child_factor.shape[1:]
    block_rows, block_cols = parent_inverse.shape
    held = block_cols // block_rows
    factor = child_factor[0]
    offsets = child_rows[0].reshape(wide, slots)
    slot_index = jnp.arange(slots, dtype=jnp.int32)
    half = width // 2
    pipe = half // PIPES
    right = [(i, i + 1) for i in range(wide - 1)]
    left = [(i + 1, i) for i in range(wide - 1)]
    ways = ((me, right, -1), (wide - 1 - me, left, 1))

    def flat(x):
        return with_layout_constraint(x, Layout(major_to_minor=(0, 1)))

    spread = [flat(factor[:, p * pipe : (p + 1) * pipe]) for p in range(PIPES)]
    summed = factor[:, half:]
    got = [[flat(lax.ppermute(spread[p], "wide", perm)) for _, perm, _ in ways] for p in range(PIPES)]

    mine = lax.dynamic_index_in_dim(offsets, me, 0, keepdims=False)
    live_mine = slot_index < lax.dynamic_index_in_dim(row_counts[0], me, 0, keepdims=False)
    flip = jnp.where(me < wide // 2, held - 1, 0)
    at = jnp.stack([jnp.where(flip > 0, held - 1 - i, i) for i in range(held)]).astype(jnp.int32)
    block = my_col * held + at
    wanted = jnp.where(slot_index[None, :] < row_counts[0][block][:, None], offsets[block], -1)
    pieces = []
    for i in range(held):
        local = pl.pallas_call(
            pick_kernel,
            out_shape=jax.ShapeDtypeStruct((slots, slots), jnp.float32),
            in_specs=[
                pl.BlockSpec(memory_space=pltpu.SMEM),
                pl.BlockSpec(memory_space=pltpu.SMEM),
                pl.BlockSpec(memory_space=pltpu.VMEM),
                pl.BlockSpec(memory_space=pltpu.VMEM),
            ]
            + [pl.BlockSpec(memory_space=pl.ANY)] * (1 + PIPES),
            out_specs=pl.BlockSpec(memory_space=pltpu.VMEM),
            scratch_shapes=[pltpu.VMEM((slots, block_rows), jnp.float32), pltpu.SemaphoreType.DMA],
            compiler_params=pltpu.CompilerParams(vmem_limit_bytes=32 * 1024 * 1024),
            cost_estimate=pl.CostEstimate(flops=1000, bytes_accessed=1000, transcendentals=0),
            name="pick",
        )(
            at[i : i + 1],
            mine,
            live_mine.astype(jnp.float32)[:, None],
            wanted[i : i + 1],
            parent_inverse,
            *spread,
        )
        pieces.append(lax.all_gather(local, "col", axis=0))
    blocks = jnp.concatenate(pieces, axis=0)

    def sigma(block):
        block = jnp.clip(block, 0, wide - 1)
        at = block % held
        order = jnp.where(flip > 0, held - 1 - at, at)
        return lax.dynamic_index_in_dim(blocks, order * cols + block // held, 0, keepdims=False)

    own = sigma(me)
    total = [dot(own, spread[p], ((1,), (0,))) for p in range(PIPES)]
    finish = dot(own, summed, ((1,), (0,)))
    for step in range(2, wide + 1):
        for w, (rank, perm, sign) in enumerate(ways):
            here = sigma(me + sign * (step - 1))
            target = me - sign * (wide - step + 1)
            if step == 2:
                owner = jnp.clip(target, 0, wide - 1) // held
                away = lax.dynamic_index_in_dim(pieces[0], owner, 0, keepdims=False)
            else:
                away = sigma(target)
            for p in range(PIPES):
                came = got[p][w]
                term = dot(away, summed[:, p * pipe : (p + 1) * pipe], ((0,), (0,)))
                send = flat(came + jnp.where(rank <= step - 2, term, 0.0))
                got[p][w] = flat(lax.ppermute(send, "wide", perm))
                total[p] += jnp.where(rank >= step - 1, dot(here, came, ((1,), (0,))), 0.0)
    parts = [-t for t in total]
    for p in range(PIPES):
        parts.append(-(finish[:, p * pipe : (p + 1) * pipe] + got[p][0] + got[p][1]))
    cross_part = jnp.concatenate(parts, axis=1)
    partial_value = jnp.sum(factor * cross_part, axis=0)
    totals = lax.psum(partial_value, "wide")
    return (cross_part[None], (own_variance[0] - totals)[None])


def solution(mesh):
    placed = (
        P(("parts", "wide"), "col"),
        P(("parts", "sub"), None),
        P(("parts", "sub"), None),
        P(("parts", "sub"), "wide", "col"),
        P(("parts", "sub"), "col"),
    )
    return jax.shard_map(
        per_device,
        mesh=mesh,
        in_specs=placed,
        out_specs=(P(("parts", "sub"), "wide", "col"), P(("parts", "sub"), "col")),
        check_vma=False,
    )
```

```python
import functools

import jax
import jax.numpy as jnp
from jax import lax
from jax.experimental import pallas as pl
from jax.experimental.pallas import tpu as pltpu
from jax.experimental.layout import Layout, with_layout_constraint
from jax.sharding import PartitionSpec as P

PIPES = 2


def pick_kernel(at_ref, mine_ref, live_ref, wanted_ref, parent_ref, *rest):
    out, rows, sem = rest[-3:]
    slots, block_rows = rows.shape
    columns = pl.ds(pl.multiple_of(at_ref[0] * block_rows, 128), block_rows)

    def issue(i, carry):
        pltpu.make_async_copy(
            parent_ref.at[pl.ds(mine_ref[i], 1), columns], rows.at[pl.ds(i, 1)], sem
        ).start()
        return carry

    lax.fori_loop(0, slots, issue, 0, unroll=8)
    pltpu.make_async_copy(parent_ref.at[pl.ds(0, slots), columns], rows, sem).wait()
    depth = 512 if block_rows % 512 == 0 else block_rows
    out[...] = jnp.zeros_like(out)

    def add(c, carry):
        x = rows[:, pl.ds(pl.multiple_of(c * depth, 128), depth)]
        high = x.astype(jnp.bfloat16)
        low = (x - high.astype(jnp.float32)).astype(jnp.bfloat16)
        place = lax.broadcasted_iota(jnp.int32, (depth, slots), 0) + c * depth
        pick = jnp.where(place == wanted_ref[...], 1.0, 0.0).astype(jnp.bfloat16)
        out[...] += jnp.dot(low, pick, preferred_element_type=jnp.float32) + jnp.dot(
            high, pick, preferred_element_type=jnp.float32
        )
        return carry

    lax.fori_loop(0, block_rows // depth, add, 0)
    out[...] = jnp.where(live_ref[...] > 0.0, out[...], 0.0)


def dot(a, b, contract):
    return lax.dot_general(
        a,
        b,
        ((contract[0], contract[1]), ((), ())),
        precision=lax.Precision.HIGH,
        preferred_element_type=jnp.float32,
    )


def per_device(parent_inverse, child_rows, row_counts, child_factor, own_variance):
    wide = lax.axis_size("wide")
    cols = lax.axis_size("col")
    me = lax.axis_index("wide")
    my_col = lax.axis_index("col")
    slots, width = child_factor.shape[1:]
    block_rows, block_cols = parent_inverse.shape
    held = block_cols // block_rows
    factor = child_factor[0]
    offsets = child_rows[0].reshape(wide, slots)
    slot_index = jnp.arange(slots, dtype=jnp.int32)
    half = width // 2
    pipe = half // PIPES
    right = [(i, i + 1) for i in range(wide - 1)]
    left = [(i + 1, i) for i in range(wide - 1)]
    ways = ((me, right, -1), (wide - 1 - me, left, 1))

    def flat(x):
        return with_layout_constraint(x, Layout(major_to_minor=(0, 1)))

    spread = [flat(factor[:, p * pipe : (p + 1) * pipe]) for p in range(PIPES)]
    summed = factor[:, half:]
    got = [[flat(lax.ppermute(spread[p], "wide", perm)) for _, perm, _ in ways] for p in range(PIPES)]

    mine = lax.dynamic_index_in_dim(offsets, me, 0, keepdims=False)
    live_mine = slot_index < lax.dynamic_index_in_dim(row_counts[0], me, 0, keepdims=False)
    flip = jnp.where(me < wide // 2, held - 1, 0)
    at = jnp.stack([jnp.where(flip > 0, held - 1 - i, i) for i in range(held)]).astype(jnp.int32)
    block = my_col * held + at
    wanted = jnp.where(slot_index[None, :] < row_counts[0][block][:, None], offsets[block], -1)
    pieces = []
    for i in range(held):
        local = pl.pallas_call(
            pick_kernel,
            out_shape=jax.ShapeDtypeStruct((slots, slots), jnp.float32),
            in_specs=[
                pl.BlockSpec(memory_space=pltpu.SMEM),
                pl.BlockSpec(memory_space=pltpu.SMEM),
                pl.BlockSpec(memory_space=pltpu.VMEM),
                pl.BlockSpec(memory_space=pltpu.VMEM),
            ]
            + [pl.BlockSpec(memory_space=pl.ANY)] * (1 + PIPES),
            out_specs=pl.BlockSpec(memory_space=pltpu.VMEM),
            scratch_shapes=[pltpu.VMEM((slots, block_rows), jnp.float32), pltpu.SemaphoreType.DMA],
            compiler_params=pltpu.CompilerParams(vmem_limit_bytes=32 * 1024 * 1024),
            cost_estimate=pl.CostEstimate(flops=1000, bytes_accessed=1000, transcendentals=0),
            name="pick",
        )(
            at[i : i + 1],
            mine,
            live_mine.astype(jnp.float32)[:, None],
            wanted[i : i + 1],
            parent_inverse,
            *spread,
        )
        if i == 1:
            corner = sum(jnp.abs(x[0, 0]) for x in got[0])
            corner = jnp.minimum(corner.astype(jnp.int32), 0)
            local = jnp.where(corner >= 0, local, 0.0)
        pieces.append(lax.all_gather(local, "col", axis=0))
    blocks = jnp.concatenate(pieces, axis=0)

    def sigma(block):
        block = jnp.clip(block, 0, wide - 1)
        at = block % held
        order = jnp.where(flip > 0, held - 1 - at, at)
        return lax.dynamic_index_in_dim(blocks, order * cols + block // held, 0, keepdims=False)

    own = sigma(me)
    total = [dot(own, spread[p], ((1,), (0,))) for p in range(PIPES)]
    finish = dot(own, summed, ((1,), (0,)))
    for step in range(2, wide + 1):
        for w, (rank, perm, sign) in enumerate(ways):
            here = sigma(me + sign * (step - 1))
            target = me - sign * (wide - step + 1)
            if step == 2:
                owner = jnp.clip(target, 0, wide - 1) // held
                away = lax.dynamic_index_in_dim(pieces[0], owner, 0, keepdims=False)
            else:
                away = sigma(target)
            for p in range(PIPES):
                came = got[p][w]
                term = dot(away, summed[:, p * pipe : (p + 1) * pipe], ((0,), (0,)))
                send = flat(came + jnp.where(rank <= step - 2, term, 0.0))
                got[p][w] = flat(lax.ppermute(send, "wide", perm))
                total[p] += jnp.where(rank >= step - 1, dot(here, came, ((1,), (0,))), 0.0)
    parts = [-t for t in total]
    for p in range(PIPES):
        parts.append(-(finish[:, p * pipe : (p + 1) * pipe] + got[p][0] + got[p][1]))
    cross_part = jnp.concatenate(parts, axis=1)
    partial_value = jnp.sum(factor * cross_part, axis=0)
    totals = lax.psum(partial_value, "wide")
    return (cross_part[None], (own_variance[0] - totals)[None])


def solution(mesh):
    placed = (
        P(("parts", "wide"), "col"),
        P(("parts", "sub"), None),
        P(("parts", "sub"), None),
        P(("parts", "sub"), "wide", "col"),
        P(("parts", "sub"), "col"),
    )
    return jax.shard_map(
        per_device,
        mesh=mesh,
        in_specs=placed,
        out_specs=(P(("parts", "sub"), "wide", "col"), P(("parts", "sub"), "col")),
        check_vma=False,
    )
```
